128 devices in a mesh: slab: 32 (over x, y, core), tile: 4 (over z).
Axes of the slice: x: 4, y: 4, z: 4, core: 2. Of those that a mesh axis runs over, the one named last changes fastest.
Arguments:
- frames: bfloat16 [128, 64, 256, 128], P('slab', 'tile'), may hold values from -21 to 21
- clip_frames: int32 [16], replicated, may hold values from 1 to 49, 128 in all
- norm_gain: float32 [128], replicated, may hold values from 0.1 to 1.9
- norm_bias: float32 [128], replicated, may hold values from -3 to 3
- conv_weight: bfloat16 [3, 3, 3, 128, 128], replicated, may hold values from -0.109375 to 0.109375
- conv_bias: float32 [128], replicated, may hold values from -3 to 3
- down_weight: bfloat16 [3, 3, 128, 128], replicated, may hold values from -0.1875 to 0.1875
- down_bias: float32 [128], replicated, may hold values from -3 to 3
Outputs:
- latent: bfloat16 [128, 32, 128, 128], P('slab', 'tile')
The draws below stay inside these ranges and needn't reach their ends.
Inputs may be any that keep to these rules, and one draw needn't show every extreme that they name: `clip_frames`: frame counts of the 16 clips of the pack, in frame order; they sum to 128.
All inputs are finite; a program needn't handle non-finite values.
Results may differ from the reference program's by a relative error of at most 0.005.
Values may be sent and summed in bfloat16 or wider, within the bound.
No kernel may reach another device: no remote copies, remote signals or barrier semaphores. Data moves between devices by JAX's collectives and lax.ppermute only.
A program may use at most 128 MiB of HBM per device.

```python
import math
import jax
import jax.numpy as jnp
import numpy as np
from jax import lax

CHANNELS = 128
GROUPS = 32
WIDTH = 256
FRAMES = 128
HEIGHT = 64
NCLIP = 16
MOST = 49


def draw_frames(key, part):
    key = jax.random.fold_in(key, 11)
    keys = jax.random.split(key, 6)
    frame_scale = jnp.exp(jax.random.uniform(keys[0], (FRAMES, 1, 1, 1), jnp.float32, -0.3, 0.3))
    channel_scale = jnp.exp(jax.random.uniform(keys[1], (1, 1, 1, CHANNELS), jnp.float32, -0.3, 0.3))
    row_scale = jnp.exp(jax.random.uniform(keys[4], (1, HEIGHT, 1, 1), jnp.float32, -1.15, 1.15))
    row_offset = jnp.clip(jax.random.normal(keys[5], (1, HEIGHT, 1, 1), jnp.float32), -2.0, 2.0) * 0.5
    noise = jnp.clip(jax.random.normal(keys[2], (FRAMES, HEIGHT, WIDTH, CHANNELS), jnp.float32), -3.0, 3.0)
    noise = noise * row_scale
    values = (noise + row_offset) * frame_scale * channel_scale
    return jnp.clip(values, -21.0, 21.0).astype(jnp.bfloat16)


def split_up(count, total, limit, skew):
    loads = [(1 << 20) // math.isqrt(rank ** skew) + 1 for rank in range(2, count + 1)]
    spare, given = total - limit - (count - 1), [1] * (count - 1)
    while spare > 0:
        candidates = [i for i in range(count - 1) if given[i] < limit]
        whole, left = sum([loads[i] for i in candidates]), spare
        for i in candidates:
            extra = min(limit - given[i], max(1, left * loads[i] // whole), spare)
            given[i] = given[i] + extra
            spare = spare - extra
    return np.array([limit] + given)


def ragged_sizes(rng, amount, total, most, slope):
    if amount == 2:
        one = jax.random.randint(rng, (), max(1, total - most), min(most, total - 1) + 1)
        return jnp.stack([one, total - one])
    tallies = jnp.asarray(split_up(amount, total, most, slope), jnp.int32)
    couples = (amount - 1) // 2
    giver, taker = tallies[1:1 + 2 * couples:2], tallies[2:2 + 2 * couples:2]
    room = jnp.minimum(giver - 1, most - taker)
    passed = jax.random.randint(jax.random.fold_in(rng, 1), (couples,), 0, 1 << 20) % (room + 1)
    tallies = tallies.at[1:1 + 2 * couples:2].set(giver - passed).at[2:2 + 2 * couples:2].set(taker + passed)
    return tallies[jax.random.permutation(jax.random.fold_in(rng, 2), amount)]


def bell_draw(own_key, shape, spread, most, kind=jnp.bfloat16):
    values = spread * jax.random.normal(own_key, shape, jnp.float32)
    return jnp.clip(values, min=-most, max=most).astype(kind)


def setup_inputs(seed: int = 0) -> dict:
    arg_keys = jax.random.split(jax.random.key(seed), 9)
    frames = draw_frames(jax.random.fold_in(arg_keys[8], 71), 0)
    clip_frames = ragged_sizes(arg_keys[1], NCLIP, FRAMES, MOST, 2).astype(jnp.int32)
    norm_gain = jnp.clip(1.0 + 0.18 * jax.random.normal(arg_keys[2], (CHANNELS,), jnp.float32), 0.1, 1.9)
    norm_bias = bell_draw(arg_keys[3], (CHANNELS,), 0.5, 3.0, jnp.float32)
    conv_weight = bell_draw(arg_keys[4], (3, 3, 3, CHANNELS, CHANNELS), (27 * CHANNELS) ** -0.5, 0.109375)
    conv_bias = bell_draw(arg_keys[5], (CHANNELS,), 0.5, 3.0, jnp.float32)
    down_weight = bell_draw(arg_keys[6], (3, 3, CHANNELS, CHANNELS), (9 * CHANNELS) ** -0.5, 0.1875)
    down_bias = bell_draw(arg_keys[7], (CHANNELS,), 0.5, 3.0, jnp.float32)
    return dict(frames=frames, clip_frames=clip_frames, norm_gain=norm_gain, norm_bias=norm_bias, conv_weight=conv_weight, conv_bias=conv_bias, down_weight=down_weight, down_bias=down_bias)


NUMBERS = ('NHWC', 'HWIO', 'NHWC')
EPSILON = 1e-06

def plane_conv(inputs, kernel, strides, padding):
    return lax.conv_general_dilated(inputs, kernel, strides, padding, dimension_numbers=NUMBERS, preferred_element_type=jnp.float32)

def group_sums(frames, groups):
    count, rows, cols, chans = frames.shape
    total = lax.optimization_barrier(jnp.sum(frames, axis=(1, 2), dtype=jnp.float32))
    square = lax.optimization_barrier(jnp.sum(jnp.square(frames.astype(jnp.float32)), axis=(1, 2)))
    total = total.reshape(count, groups, chans // groups).sum(-1)
    square = square.reshape(count, groups, chans // groups).sum(-1)
    return (total, square)

def reference(frames, clip_frames, norm_gain, norm_bias, conv_weight, conv_bias, down_weight, down_bias):
    ends = jnp.cumsum(clip_frames).astype(jnp.int32)
    starts = (ends - clip_frames).astype(jnp.int32)
    frame_index = jnp.arange(FRAMES, dtype=jnp.int32)
    member = (frame_index[:, None] >= starts[None, :]) & (frame_index[:, None] < ends[None, :])
    clip_start = lax.optimization_barrier(jnp.sum(jnp.where(member, starts[None, :], 0), axis=1)).astype(jnp.int32)
    onehot = member.astype(jnp.float32)
    total, square = group_sums(frames, GROUPS)
    one_sum = jnp.dot(onehot.T, total, precision=lax.Precision.HIGHEST)
    two_sum = jnp.dot(onehot.T, square, precision=lax.Precision.HIGHEST)
    counts = clip_frames.astype(jnp.float32) * (HEIGHT * WIDTH * (CHANNELS // GROUPS))
    mean = one_sum / counts[:, None]
    variance = two_sum / counts[:, None] - mean * mean
    inverse = lax.rsqrt(variance + EPSILON)
    frame_mean = jnp.repeat(jnp.dot(onehot, mean, precision=lax.Precision.HIGHEST), CHANNELS // GROUPS, axis=1)
    frame_inverse = jnp.repeat(jnp.dot(onehot, inverse, precision=lax.Precision.HIGHEST), CHANNELS // GROUPS, axis=1)
    scale = norm_gain[None, :] * frame_inverse
    shift = norm_bias[None, :] - frame_mean * scale
    act = jax.nn.silu(frames.astype(jnp.float32) * scale[:, None, None, :] + shift[:, None, None, :]).astype(jnp.bfloat16)

    def one_frame(frame):
        total_conv = jnp.zeros((1, HEIGHT, WIDTH, CHANNELS), jnp.float32) + conv_bias
        for tap_time in range(3):
            source = jnp.maximum(frame + tap_time - 2, clip_start[frame]).astype(jnp.int32)
            plane = lax.dynamic_index_in_dim(act, source, 0, keepdims=True)
            total_conv = total_conv + plane_conv(plane, conv_weight[tap_time], (1, 1), ((1, 1), (1, 1)))
        own = lax.dynamic_index_in_dim(frames, frame, 0, keepdims=True)
        mixed = (own.astype(jnp.float32) + total_conv).astype(jnp.bfloat16)
        padded = jnp.pad(mixed, ((0, 0), (0, 1), (0, 1), (0, 0)))
        result = plane_conv(padded, down_weight, (2, 2), 'VALID') + down_bias
        return result[0].astype(jnp.bfloat16)
    return lax.map(one_frame, frame_index)
```

```python
import functools

import jax
import jax.numpy as jnp
from jax import lax
from jax.experimental import pallas as pl
from jax.experimental.pallas import tpu as pltpu
from jax.sharding import PartitionSpec as P

GROUPS = 32
EPSILON = 1e-06
VMEM_LIMIT = 60 * 1024 * 1024
HIGHEST = lax.Precision.HIGHEST
F32 = jnp.float32
BF16 = jnp.bfloat16


def sums_kernel(steps, x_ref, out_ref, acc):
    frame, part = pl.program_id(0), pl.program_id(1)
    rows, cols, chans = x_ref.shape[1:]
    x = x_ref[0].reshape(rows * cols // 64, 64, chans).astype(F32)
    one = jnp.sum(x, axis=0)
    two = jnp.sum(x * x, axis=0)

    @pl.when(part == 0)
    def _():
        acc[frame, 0] = one
        acc[frame, 1] = two

    @pl.when(part > 0)
    def _():
        acc[frame, 0] += one
        acc[frame, 1] += two

    @pl.when((frame == pl.num_programs(0) - 1) & (part == steps - 1))
    def _():
        both = [
            jnp.concatenate([jnp.sum(acc[f, i], axis=0, keepdims=True) for f in range(4)], axis=1)
            for i in range(2)
        ]
        row = lax.broadcasted_iota(jnp.int32, (4 * chans, chans), 0)
        lane = lax.broadcasted_iota(jnp.int32, (4 * chans, chans), 1)
        member = ((row >> 2) == lane).astype(F32)
        sums = jnp.dot(jnp.concatenate(both, axis=0), member, precision=HIGHEST, preferred_element_type=F32)
        out_ref[...] = jnp.broadcast_to(sums[None], out_ref.shape)


def frame_sums(frames, devices):
    count, rows, cols, chans = frames.shape
    steps = 2
    return pl.pallas_call(
        functools.partial(sums_kernel, steps),
        grid=(count, steps),
        in_specs=[pl.BlockSpec((1, rows // steps, cols, chans), lambda f, p: (f, p, 0, 0))],
        out_specs=pl.BlockSpec((devices, 2, chans), lambda f, p: (0, 0, 0)),
        out_shape=jax.ShapeDtypeStruct((devices, 2, chans), F32),
        scratch_shapes=[pltpu.VMEM((count, 2, 64, chans), F32)],
        compiler_params=pltpu.CompilerParams(vmem_limit_bytes=VMEM_LIMIT),
        name="frame_sums",
    )(frames)


def own_rows(step):
    if step == 0:
        return 0, 3
    if step < 7:
        return 2 * step + 1, 2
    return 15, 1


def block_kernel(
    cfg, pos_ref, clips_ref, sums_ref, gain_ref, bias_ref, w_ref, cb_ref, dw_ref, db_ref,
    early, late, top_early, top_late, bot_early, bot_late, *rest,
):
    base, e0, l0, o0, aliased = cfg
    if aliased:
        rest = rest[1:]
    out_ref, xin, xs, wa, wbe, wbo, wd, vsum, obuf, sems, osems = rest[:11]
    act = rest[11:30]
    res = rest[30:47]
    mix = rest[47:64]
    count = 4
    slab, tile, tiles = pos_ref[0], pos_ref[1], pos_ref[2]

    copies = {}
    used = [0]

    def start(step, src, dst):
        copy = pltpu.make_async_copy(src, dst, sems.at[used[0]])
        used[0] += 1
        copy.start()
        copies.setdefault(step, []).append(copy)

    for s in range(9):
        if s == 0:
            for src, b, slot in ((top_early, e0, 0), (top_late, l0, 2)):
                start(0, src.at[pl.ds(b, 2), pl.ds(0, 1)], xin.at[pl.ds(slot, 2), pl.ds(0, 1)])
        if s < 8:
            lo, n = own_rows(s)
            for src, b, slot in ((early, e0, 0), (late, l0, 2)):
                start(s, src.at[pl.ds(b, 2), pl.ds(lo, n)], xin.at[pl.ds(slot, 2), pl.ds(lo + 1, n)])
        if s >= 7:
            for src, b, slot in ((bot_early, e0, 0), (bot_late, l0, 2)):
                start(s, src.at[pl.ds(b, 2), pl.ds(s - 7, 1)], xin.at[pl.ds(slot, 2), pl.ds(s + 10, 1)])

    first = slab * count + base
    starts = [jnp.int32(0)] * 4
    ends = [jnp.int32(1)] * 4
    begin = jnp.int32(0)
    for c in range(clips_ref.shape[0]):
        end = begin + clips_ref[c]
        for f in range(4):
            inside = (begin <= first + f) & (first + f < end)
            starts[f] = jnp.where(inside, begin, starts[f])
            ends[f] = jnp.where(inside, end, ends[f])
        begin = end
    source = [[jnp.maximum(first + t + k - 2, starts[t]) - first for k in range(3)] for t in (2, 3)]

    slabs = sums_ref.shape[0] // 4
    sums = jnp.sum(sums_ref[...].reshape(slabs, 4, 2, 128), axis=1)
    frame_of = 4 * lax.broadcasted_iota(jnp.int32, (slabs, 2, 128), 0) + (
        lax.broadcasted_iota(jnp.int32, (slabs, 2, 128), 2) >> 5
    )
    for f in range(4):
        inside = (frame_of >= starts[f]) & (frame_of < ends[f])
        vsum[2 * f:2 * f + 2, :] = jnp.sum(jnp.where(inside, sums, 0.0), axis=0)
    group = lax.broadcasted_iota(jnp.int32, (128, 128), 0) & (GROUPS - 1)
    chan = lax.broadcasted_iota(jnp.int32, (128, 128), 1) >> 2
    totals = jnp.dot(vsum[...], (group == chan).astype(F32), precision=HIGHEST, preferred_element_type=F32)
    half_scale, half_shift = [], []
    for f in range(4):
        pixels = (ends[f] - starts[f]) * (tiles * 16 * 256 * 4)
        number = jnp.full((1, 128), pixels, jnp.int32).astype(F32)
        mean = totals[2 * f:2 * f + 1] / number
        variance = totals[2 * f + 1:2 * f + 2] / number - mean * mean
        scale = gain_ref[...] * lax.rsqrt(variance + EPSILON)
        half_scale.append(0.5 * scale)
        half_shift.append(0.5 * (bias_ref[...] - mean * scale))

    zero = jnp.zeros((128, 128), BF16)
    for k in range(3):
        for dy in range(3):
            w0, w1, w2 = (w_ref[k, dy, dx] for dx in range(3))
            r = (dy * 3 + k) * 256
            wa[r:r + 128, 0:128] = w1
            wa[r:r + 128, 128:256] = w0
            wa[r + 128:r + 256, 0:128] = w2
            wa[r + 128:r + 256, 128:256] = w1
            for wb, w in ((wbe, w0), (wbo, w2)):
                a = (dy * 3 + k) * 128
                b = ((dy + 1) * 3 + k) * 128
                wb[a:a + 128, 0:128] = w
                wb[b:b + 128, 128:256] = w
        for wb in (wbe, wbo):
            wb[k * 128:(k + 1) * 128, 128:256] = zero
            wb[(9 + k) * 128:(10 + k) * 128, 0:128] = zero
    for dy in range(3):
        r = dy * 256
        wd[r:r + 128, 0:128] = dw_ref[dy, 0]
        wd[r + 128:r + 256, 0:128] = dw_ref[dy, 1]
        wd[r:r + 128, 128:256] = dw_ref[dy, 2]
        wd[r + 128:r + 256, 128:256] = zero

    def activate(idx, f, slot):
        xs[slot] = xin[f, idx].astype(F32)
        for p in range(2):
            lanes = slice(p * 128, (p + 1) * 128)
            v = xs[slot, pl.ds(p, 128, stride=2), :]
            if f >= 2 and 1 <= idx <= 17:
                res[idx - 1][f - 2, :, lanes] = v.astype(BF16)
            u = v * half_scale[f] + half_shift[f]
            a = u + u * jnp.tanh(u)
            if idx == 0:
                a = jnp.where(tile == 0, 0.0, a)
            if idx >= 17:
                a = jnp.where(tile == tiles - 1, 0.0, a)
            act[idx][f, :, lanes] = a.astype(BF16)

    def act_step(s):
        if s > 8:
            return
        for copy in copies[s]:
            copy.wait()
        rows = [0, 1, 2, 3] if s == 0 else ([2 * s + 2, 2 * s + 3] if s < 8 else [18])
        for i, idx in enumerate(rows):
            for f in range(4):
                activate(idx, f, (s % 2) * 16 + i * 4 + f)

    pair = lax.broadcasted_iota(jnp.int32, (128, 128), 0)

    def from_before(p):
        return jnp.where(pair == 0, 0.0, pltpu.roll(p, 1, 0))

    def from_after(p):
        return jnp.where(pair == 127, 0.0, pltpu.roll(p, 127, 0))

    cb = jnp.concatenate([cb_ref[...], cb_ref[...]], axis=1)

    def dot(a, b):
        return jnp.dot(a, b, preferred_element_type=F32)

    def finish(y, t, own, even, odd):
        m = res[y][t].astype(F32) + cb + own
        for p, v in ((0, m[:, :128] + from_before(even)), (1, m[:, 128:] + from_after(odd))):
            if y == 16:
                v = jnp.where(tile == tiles - 1, 0.0, v)
            mix[y][t, :, p * 128:(p + 1) * 128] = v.astype(BF16)

    def conv_step(s):
        y = 2 * s
        n = 1 if s == 8 else 2
        blocks = []
        for t in range(2):
            for i in range(n):
                blocks.append(jnp.concatenate(
                    [act[y + i + dy][source[t][k]] for dy in range(3) for k in range(3)], axis=1))
        own = dot(jnp.concatenate(blocks, axis=0), wa[...])
        sides = []
        for p, wb in ((1, wbe), (0, wbo)):
            left = jnp.concatenate([
                jnp.concatenate(
                    [act[y + q][source[t][k], :, p * 128:(p + 1) * 128] for q in range(n + 2) for k in range(3)],
                    axis=1)
                for t in range(2)], axis=0)
            sides.append(dot(left, wb[...] if n == 2 else wb[0:1152, 0:128]))
        for t in range(2):
            for i in range(n):
                m = (t * n + i) * 128
                even, odd = (v[t * 128:(t + 1) * 128, i * 128:(i + 1) * 128] for v in sides)
                finish(y + i, t, own[m:m + 128], even, odd)

    outs = []

    def out_row(r):
        left = jnp.concatenate(
            [jnp.concatenate([mix[2 * r + dy][t] for dy in range(3)], axis=1) for t in range(2)], axis=0)
        p = dot(left, wd[...])
        for t in range(2):
            q = p[t * 128:(t + 1) * 128]
            obuf[r, t, 0] = (q[:, :128] + from_after(q[:, 128:]) + db_ref[...]).astype(BF16)
        copy = pltpu.make_async_copy(obuf.at[r], out_ref.at[pl.ds(o0, 2), pl.ds(r, 1)], osems.at[r])
        copy.start()
        outs.append(copy)

    act_step(0)
    for s in range(9):
        conv_step(s)
        act_step(s + 1)
        if s >= 1:
            out_row(s - 1)
    for copy in outs:
        copy.wait()


def two_frames(cfg, small, big, before=None):
    anywhere = pl.BlockSpec(memory_space=pl.ANY)
    vmem = pl.BlockSpec(memory_space=pltpu.VMEM)
    smem = pl.BlockSpec(memory_space=pltpu.SMEM)
    scratch = [
        pltpu.VMEM((4, 19, 256, 128), BF16),
        pltpu.VMEM((32, 256, 128), F32),
        pltpu.VMEM((2304, 256), BF16),
        pltpu.VMEM((1536, 256), BF16),
        pltpu.VMEM((1536, 256), BF16),
        pltpu.VMEM((768, 256), BF16),
        pltpu.VMEM((8, 128), F32),
        pltpu.VMEM((8, 2, 1, 128, 128), BF16),
        pltpu.SemaphoreType.DMA((22,)),
        pltpu.SemaphoreType.DMA((8,)),
    ]
    scratch += [pltpu.VMEM((4, 128, 256), BF16)] * 19
    scratch += [pltpu.VMEM((2, 128, 256), BF16)] * 34
    operands = list(small) + list(big)
    specs = [smem, smem] + [vmem] * 7 + [anywhere] * 6
    aliases = {}
    if before is not None:
        aliases = {len(operands): 0}
        operands.append(before)
        specs.append(anywhere)
    return pl.pallas_call(
        functools.partial(block_kernel, cfg + (before is not None,)),
        out_shape=jax.ShapeDtypeStruct((4, 8, 128, 128), BF16),
        in_specs=specs,
        out_specs=anywhere,
        scratch_shapes=scratch,
        input_output_aliases=aliases,
        compiler_params=pltpu.CompilerParams(vmem_limit_bytes=VMEM_LIMIT),
        cost_estimate=pl.CostEstimate(flops=16 * 10**9, bytes_accessed=6 * 2**20, transcendentals=10**7),
        name="two_frames",
    )(*operands)


def shards(frames, clip_frames, norm_gain, norm_bias, conv_weight, conv_bias, down_weight, down_bias):
    slabs, tiles = lax.axis_size("slab"), lax.axis_size("tile")
    both = ("slab", "tile")

    def flat(s, t):
        return s * tiles + t

    earlier = lax.ppermute(frames[2:4], "slab", [(s, s + 1) for s in range(slabs - 1)])
    top = lax.ppermute(frames[:, 15:16], "tile", [(t, t + 1) for t in range(tiles - 1)])
    bottom = lax.ppermute(frames[:, 0:2], "tile", [(t + 1, t) for t in range(tiles - 1)])
    cells = [(s, t) for s in range(slabs - 1) for t in range(tiles - 1)]
    top_earlier = lax.ppermute(frames[2:4, 15:16], both, [(flat(s, t), flat(s + 1, t + 1)) for s, t in cells])
    bottom_earlier = lax.ppermute(frames[2:4, 0:2], both, [(flat(s, t + 1), flat(s + 1, t)) for s, t in cells])

    sums = lax.all_to_all(frame_sums(frames, slabs * tiles), both, 0, 0)
    place = jnp.stack([lax.axis_index("slab"), lax.axis_index("tile"), jnp.int32(tiles)]).astype(jnp.int32)
    small = (
        place, clip_frames, sums, norm_gain[None], norm_bias[None], conv_weight, conv_bias[None], down_weight,
        down_bias[None],
    )
    last = two_frames((0, 0, 2, 2), small, (frames, frames, top, top, bottom, bottom))
    return two_frames(
        (-2, 0, 0, 0), small, (earlier, frames, top_earlier, top, bottom_earlier, bottom), before=last)


def solution(mesh):
    return jax.shard_map(
        shards,
        mesh=mesh,
        in_specs=(P("slab", "tile", None, None), P(), P(), P(), P(), P(), P(), P()),
        out_specs=P("slab", "tile", None, None),
        check_vma=False,
    )
```

```python
import functools

import jax
import jax.numpy as jnp
from jax import lax
from jax.experimental import pallas as pl
from jax.experimental.pallas import tpu as pltpu
from jax.sharding import PartitionSpec as P

GROUPS = 32
EPSILON = 1e-06
VMEM_LIMIT = 36 * 1024 * 1024
FLOPS = 200 * 10**9
F32 = jnp.float32
BF16 = jnp.bfloat16


def gathered(x, member):
    parts = []
    for _ in range(3):
        parts.append(x.astype(BF16))
        x = x - parts[-1].astype(F32)
    n = x.shape[0]
    out = jnp.dot(jnp.concatenate(parts, axis=0), member.astype(BF16), preferred_element_type=F32)
    return out[:n] + out[n:2 * n] + out[2 * n:]


def sums_kernel(pieces, x_ref, out_ref, far_ref, near_ref, top_ref, bottom_ref, corner_top_ref, corner_bottom_ref, xin, load, store):
    count, rows, cols, chans = x_ref.shape
    part = rows // pieces
    order = [2, 3, 0, 1]
    loads = {}
    for f in order:
        for p in range(pieces):
            cut = pl.ds(p * part, part)
            copy = pltpu.make_async_copy(x_ref.at[f, cut], xin.at[f, cut], load.at[f * pieces + p])
            copy.start()
            loads[f, p] = copy
    stores = []

    def send(src, dst):
        copy = pltpu.make_async_copy(src, dst, store.at[len(stores)])
        copy.start()
        stores.append(copy)

    sums = {}
    for f in order:
        one = two = jnp.zeros((32, chans), F32)
        for p in range(pieces):
            loads[f, p].wait()
            if p == pieces - 1:
                send(xin.at[f, pl.ds(0, 2)], bottom_ref.at[f])
                send(xin.at[f, pl.ds(rows - 1, 1)], top_ref.at[f])
                if f >= 2:
                    send(xin.at[f], (far_ref, near_ref)[f - 2].at[0])
                    send(xin.at[f, pl.ds(0, 2)], corner_bottom_ref.at[f - 2])
                    send(xin.at[f, pl.ds(rows - 1, 1)], corner_top_ref.at[f - 2])

            def row(i, both, f=f, p=p):
                x = xin[f, p * part + i].astype(F32).reshape(cols // 32, 32, chans)
                return both[0] + jnp.sum(x, axis=0), both[1] + jnp.sum(x * x, axis=0)

            one, two = lax.fori_loop(0, part, row, (one, two))
        sums[f] = [jnp.sum(v, axis=0, keepdims=True) for v in (one, two)]
    both = jnp.concatenate([jnp.concatenate([sums[f][i] for f in range(count)], axis=1) for i in range(2)], axis=0)
    row = lax.broadcasted_iota(jnp.int32, (4 * chans, chans), 0)
    lane = lax.broadcasted_iota(jnp.int32, (4 * chans, chans), 1)
    member = ((row >> 2) == lane).astype(F32)
    packed = gathered(both, member)
    out_ref[...] = jnp.broadcast_to(packed[None], out_ref.shape)
    for copy in stores:
        copy.wait()


def sums_and_rows(frames, devices):
    count, rows, cols, chans = frames.shape
    pieces = 4
    anywhere = pl.BlockSpec(memory_space=pl.ANY)
    shapes = [(1, rows), (1, rows), (count, 1), (count, 2), (2, 1), (2, 2)]
    return pl.pallas_call(
        functools.partial(sums_kernel, pieces),
        in_specs=[anywhere],
        out_specs=[pl.BlockSpec(memory_space=pltpu.VMEM)] + [anywhere] * 6,
        out_shape=[jax.ShapeDtypeStruct((devices, 2, chans), F32)]
        + [jax.ShapeDtypeStruct(s + (cols, chans), BF16) for s in shapes],
        scratch_shapes=[
            pltpu.VMEM((count, rows, cols, chans), BF16),
            pltpu.SemaphoreType.DMA((count * pieces,)),
            pltpu.SemaphoreType.DMA((14,)),
        ],
        compiler_params=pltpu.CompilerParams(vmem_limit_bytes=60 * 1024 * 1024),
        name="sums_and_rows",
    )(frames)


def block_kernel(
    base, target, groups, pos_ref, clips_ref, gain_ref, bias_ref, cb_ref, db_ref, sums_hbm, w_hbm, dw_hbm, *rest,
):
    inputs, rest = rest[:groups[0]], rest[groups[0]:]
    out_ref, xin, xs, wa, wbe, wbo, wd, vsum, obuf, sums_ref, w_ref, dw_ref, sems, osem = rest[:14]
    rows = rest[14:]
    act, res, mix = rows[:19], rows[19:36], rows[36:]
    count, slots = 2, 4
    slab, tile, tiles = pos_ref[0], pos_ref[1], pos_ref[2]

    copies = {}
    used = [0]

    def arrive(step):
        for copy in copies[step]:
            copy.wait()

    def start(step, src, dst):
        copy = pltpu.make_async_copy(src, dst, sems.at[used[0]])
        used[0] += 1
        copy.start()
        copies.setdefault(step, []).append(copy)

    def fetch(step, which, first_row, number, at):
        for slot, n, *places in groups[1]:
            ref, index = places[which]
            src = inputs[ref].at[pl.ds(index, n), pl.ds(first_row, number)]
            start(step, src, xin.at[pl.ds(slot, n), pl.ds(at, number)])

    start(0, sums_hbm, sums_ref)
    fetch(0, 1, 0, 1, 0)
    fetch(0, 0, 0, 3, 1)
    start(0, w_hbm, w_ref)
    start(0, dw_hbm, dw_ref)
    fetch(1, 0, 3, 13, 4)
    fetch(1, 2, 0, 2, 17)

    first = slab * 4 + base
    starts = [jnp.int32(0)] * slots
    ends = [jnp.int32(1)] * slots
    begin = jnp.int32(0)
    for c in range(clips_ref.shape[0]):
        end = begin + clips_ref[c]
        for f in range(slots):
            inside = (begin <= first + f) & (first + f < end)
            starts[f] = jnp.where(inside, begin, starts[f])
            ends[f] = jnp.where(inside, end, ends[f])
        begin = end
    opens = [starts[f] == first + f for f in range(slots)]
    second = [starts[f] == first + f - 1 for f in range(slots)]

    arrive(0)
    slabs = sums_ref.shape[0] // 4
    sums = jnp.sum(sums_ref[...].reshape(slabs, 4, 2, 128), axis=1)
    frame_of = 4 * lax.broadcasted_iota(jnp.int32, (slabs, 2, 128), 0) + (
        lax.broadcasted_iota(jnp.int32, (slabs, 2, 128), 2) >> 5
    )
    for f in range(slots):
        inside = (frame_of >= starts[f]) & (frame_of < ends[f])
        vsum[2 * f:2 * f + 2, :] = jnp.sum(jnp.where(inside, sums, 0.0), axis=0)
    group = lax.broadcasted_iota(jnp.int32, (128, 128), 0) & (GROUPS - 1)
    chan = lax.broadcasted_iota(jnp.int32, (128, 128), 1) >> 2
    totals = gathered(vsum[...], (group == chan).astype(F32))
    half_scale, half_shift = [], []
    for f in range(slots):
        pixels = (ends[f] - starts[f]) * (tiles * 16 * 256 * 4)
        number = jnp.full((1, 128), pixels, jnp.int32).astype(F32)
        mean = totals[2 * f:2 * f + 1] / number
        variance = totals[2 * f + 1:2 * f + 2] / number - mean * mean
        scale = gain_ref[...] * lax.rsqrt(variance + EPSILON)
        half_scale.append(0.5 * scale)
        half_shift.append(0.5 * (bias_ref[...] - mean * scale))

    def activate(idx, slot):
        for f in range(slots):
            xs[slot + f] = xin[f, idx].astype(F32)
        for p in range(2):
            lanes = slice(p * 128, (p + 1) * 128)
            planes = []
            for f in range(slots):
                v = xs[slot + f, pl.ds(p, 128, stride=2), :]
                if f >= 2 and 1 <= idx <= 17:
                    res[idx - 1][f - 2, :, lanes] = v.astype(BF16)
                u = v * half_scale[f] + half_shift[f]
                a = u + u * jnp.tanh(u)
                if idx == 0:
                    a = jnp.where(tile == 0, 0.0, a)
                if idx >= 17:
                    a = jnp.where(tile == tiles - 1, 0.0, a)
                planes.append(a.astype(BF16))
            for f in range(2, slots):
                now, before, oldest = planes[f], planes[f - 1], planes[f - 2]
                before = jnp.where(opens[f], now, before)
                oldest = jnp.where(opens[f] | second[f], before, oldest)
                for k, plane in enumerate((oldest, before, now)):
                    act[idx][3 * (f - 2) + k, :, lanes] = plane.astype(BF16)

    def act_step(s):
        rows = [0, 1, 2, 3] if s == 0 else ([2 * s + 2, 2 * s + 3] if s < 8 else [18])
        for i, idx in enumerate(rows):
            activate(idx, (s % 2) * 4 * slots + i * slots)

    def build_weights():
        zero = jnp.zeros((128, 128), BF16)
        for k in range(3):
            for dy in range(3):
                w0, w1, w2 = (w_ref[k, dy, dx] for dx in range(3))
                r = (dy * 3 + k) * 256
                wa[r:r + 128, 0:128] = w1
                wa[r:r + 128, 128:256] = w0
                wa[r + 128:r + 256, 0:128] = w2
                wa[r + 128:r + 256, 128:256] = w1
                for wb, w in ((wbe, w0), (wbo, w2)):
                    a = (dy * 3 + k) * 128
                    b = ((dy + 1) * 3 + k) * 128
                    wb[a:a + 128, 0:128] = w
                    wb[b:b + 128, 128:256] = w
            for wb in (wbe, wbo):
                wb[k * 128:(k + 1) * 128, 128:256] = zero
                wb[(9 + k) * 128:(10 + k) * 128, 0:128] = zero
        for dy in range(3):
            r = dy * 256
            wd[r:r + 128, 0:128] = dw_ref[dy, 0]
            wd[r + 128:r + 256, 0:128] = dw_ref[dy, 1]
            wd[r:r + 128, 128:256] = dw_ref[dy, 2]
            wd[r + 128:r + 256, 128:256] = zero

    pair = lax.broadcasted_iota(jnp.int32, (128, 128), 0)

    def from_before(p):
        return jnp.where(pair == 0, 0.0, pltpu.roll(p, 1, 0))

    def from_after(p):
        return jnp.where(pair == 127, 0.0, pltpu.roll(p, 127, 0))

    cb = jnp.concatenate([cb_ref[...], cb_ref[...]], axis=1)

    def dot(a, b):
        return jnp.dot(a, b, preferred_element_type=F32)

    def finish(y, t, own, even, odd):
        m = res[y][t].astype(F32) + cb + own
        for p, v in ((0, m[:, :128] + from_before(even)), (1, m[:, 128:] + from_after(odd))):
            if y == 16:
                v = jnp.where(tile == tiles - 1, 0.0, v)
            mix[y][t, :, p * 128:(p + 1) * 128] = v.astype(BF16)

    def conv_step(s):
        y = 2 * s
        n = 1 if s == 8 else 2
        for t in range(count):
            blocks = [
                jnp.concatenate([act[y + i + dy][3 * t + k] for dy in range(3) for k in range(3)], axis=1)
                for i in range(n)
            ]
            own = dot(jnp.concatenate(blocks, axis=0), wa[...])
            sides = []
            for p, wb in ((1, wbe), (0, wbo)):
                left = jnp.concatenate(
                    [act[y + q][3 * t + k, :, p * 128:(p + 1) * 128] for q in range(n + 2) for k in range(3)],
                    axis=1)
                sides.append(dot(left, wb[...] if n == 2 else wb[0:1152, 0:128]))
            for i in range(n):
                even, odd = (v[:, i * 128:(i + 1) * 128] for v in sides)
                finish(y + i, t, own[i * 128:(i + 1) * 128], even, odd)

    def out_row(r):
        left = jnp.concatenate(
            [jnp.concatenate([mix[2 * r + dy][t] for dy in range(3)], axis=1) for t in range(count)], axis=0)
        p = dot(left, wd[...])
        for t in range(count):
            q = p[t * 128:(t + 1) * 128]
            obuf[t, r] = (q[:, :128] + from_after(q[:, 128:]) + db_ref[...]).astype(BF16)

    act_step(0)
    build_weights()
    for s in range(9):
        conv_step(s)
        if s == 0:
            arrive(1)
        if s < 8:
            act_step(s + 1)
        if s >= 2:
            out_row(s - 2)
    out_row(7)
    copy = pltpu.make_async_copy(obuf, out_ref.at[pl.ds(target, 2)], osem)
    copy.start()
    copy.wait()


def two_frames(base, target, scalars, vectors, shared, big, groups, flops, unread):
    anywhere = pl.BlockSpec(memory_space=pl.ANY)
    vmem = pl.BlockSpec(memory_space=pltpu.VMEM)
    smem = pl.BlockSpec(memory_space=pltpu.SMEM)
    out = jax.ShapeDtypeStruct((4, 8, 128, 128), BF16)
    scratch = [
        pltpu.VMEM((4, 19, 256, 128), BF16),
        pltpu.VMEM((32, 256, 128), F32),
        pltpu.VMEM((2304, 256), BF16),
        pltpu.VMEM((1536, 256), BF16),
        pltpu.VMEM((1536, 256), BF16),
        pltpu.VMEM((768, 256), BF16),
        pltpu.VMEM((8, 128), F32),
        pltpu.VMEM((2, 8, 128, 128), BF16),
        pltpu.VMEM(shared[0].shape, F32),
        pltpu.VMEM(shared[1].shape, BF16),
        pltpu.VMEM(shared[2].shape, BF16),
        pltpu.SemaphoreType.DMA((3 + 4 * len(groups),)),
        pltpu.SemaphoreType.DMA,
    ]
    scratch += [pltpu.VMEM((6, 128, 256), BF16)] * 19
    scratch += [pltpu.VMEM((2, 128, 256), BF16)] * 34
    operands = [*scalars, *vectors, *shared, *big, *unread]
    specs = [smem] * len(scalars) + [vmem] * len(vectors) + [anywhere] * (len(shared) + len(big) + len(unread))
    return pl.pallas_call(
        functools.partial(block_kernel, base, target, (len(big) + len(unread), groups)),
        out_shape=out,
        in_specs=specs,
        out_specs=anywhere,
        scratch_shapes=scratch,
        input_output_aliases={len(operands) - 1: 0} if target == 0 else {},
        compiler_params=pltpu.CompilerParams(vmem_limit_bytes=VMEM_LIMIT),
        cost_estimate=pl.CostEstimate(flops=flops, bytes_accessed=6 * 2**20, transcendentals=10**7),
        name="two_frames",
    )(*operands)


def shards(frames, clip_frames, norm_gain, norm_bias, conv_weight, conv_bias, down_weight, down_bias):
    slabs, tiles = lax.axis_size("slab"), lax.axis_size("tile")
    both = ("slab", "tile")

    frames = pltpu.with_memory_space_constraint(frames, pltpu.HBM)

    def flat(s, t):
        return s * tiles + t

    sums, far, near, top, bottom, corner_top, corner_bottom = sums_and_rows(frames, slabs * tiles)
    sums = lax.all_to_all(sums, both, 0, 0)
    cells = [(s, t) for s in range(slabs - 1) for t in range(tiles - 1)]
    top = lax.ppermute(top, "tile", [(t, t + 1) for t in range(tiles - 1)])
    bottom = lax.ppermute(bottom, "tile", [(t + 1, t) for t in range(tiles - 1)])
    along = [(s, s + 1) for s in range(slabs - 1)]
    near = lax.ppermute(near, "slab", along)
    far = lax.ppermute(far, "slab", along)
    top_earlier = lax.ppermute(corner_top, both, [(flat(s, t), flat(s + 1, t + 1)) for s, t in cells])
    bottom_earlier = lax.ppermute(corner_bottom, both, [(flat(s, t + 1), flat(s + 1, t)) for s, t in cells])
    place = jnp.stack([lax.axis_index("slab"), lax.axis_index("tile"), jnp.int32(tiles)]).astype(jnp.int32)
    vectors = [v[None] for v in (norm_gain, norm_bias, conv_bias, down_bias)]
    scalars, shared = (place, clip_frames), (sums, conv_weight, down_weight)
    last = two_frames(
        0, 2, scalars, vectors, shared, (frames, top, bottom), [(0, 4, (0, 0), (1, 0), (2, 0))], FLOPS, (near,))
    groups = [
        (0, 1, (0, 0), (1, 0), (2, 0)),
        (1, 1, (3, 0), (1, 1), (2, 1)),
        (2, 2, (4, 0), (5, 0), (6, 0)),
    ]
    return two_frames(
        -2, 0, scalars, vectors, shared, (far, top_earlier, bottom_earlier, near, frames, top, bottom), groups, FLOPS,
        (last,))


def solution(mesh):
    return jax.shard_map(
        shards,
        mesh=mesh,
        in_specs=(P("slab", "tile", None, None), P(), P(), P(), P(), P(), P(), P()),
        out_specs=P("slab", "tile", None, None),
        check_vma=False,
    )
```

```python
import functools

import jax
import jax.numpy as jnp
from jax import lax
from jax.experimental import pallas as pl
from jax.experimental.pallas import tpu as pltpu
from jax.sharding import PartitionSpec as P

GROUPS = 32
EPSILON = 1e-06
VMEM_LIMIT = 36 * 1024 * 1024
FLOPS = 200 * 10**9
F32 = jnp.float32
BF16 = jnp.bfloat16


def gathered(x, member):
    parts = []
    for _ in range(3):
        parts.append(x.astype(BF16))
        x = x - parts[-1].astype(F32)
    n = x.shape[0]
    out = jnp.dot(jnp.concatenate(parts, axis=0), member.astype(BF16), preferred_element_type=F32)
    return out[:n] + out[n:2 * n] + out[2 * n:]


def sums_kernel(pieces, x_ref, out_ref, far_ref, near_ref, top_ref, bottom_ref, xin, load, store):
    count, rows, cols, chans = x_ref.shape
    part = rows // pieces
    order = [2, 3, 0, 1]
    loads = {}
    for f in order:
        for p in range(pieces):
            cut = pl.ds(p * part, part)
            copy = pltpu.make_async_copy(x_ref.at[f, cut], xin.at[f, cut], load.at[f * pieces + p])
            copy.start()
            loads[f, p] = copy
    stores = []

    def send(src, dst):
        copy = pltpu.make_async_copy(src, dst, store.at[len(stores)])
        copy.start()
        stores.append(copy)

    sums = {}
    for f in order:
        one = two = jnp.zeros((32, chans), F32)
        for p in range(pieces):
            loads[f, p].wait()
            if p == pieces - 1:
                send(xin.at[f, pl.ds(0, 2)], bottom_ref.at[f])
                send(xin.at[f, pl.ds(rows - 1, 1)], top_ref.at[f])
                if f >= 2:
                    send(xin.at[f], (far_ref.at[0, pl.ds(0, rows)], near_ref.at[0])[f - 2])

            def row(i, both, f=f, p=p):
                x = xin[f, p * part + i].astype(F32).reshape(cols // 32, 32, chans)
                return both[0] + jnp.sum(x, axis=0), both[1] + jnp.sum(x * x, axis=0)

            one, two = lax.fori_loop(0, part, row, (one, two))
        sums[f] = [jnp.sum(v, axis=0, keepdims=True) for v in (one, two)]
    both = jnp.concatenate([jnp.concatenate([sums[f][i] for f in range(count)], axis=1) for i in range(2)], axis=0)
    row = lax.broadcasted_iota(jnp.int32, (4 * chans, chans), 0)
    lane = lax.broadcasted_iota(jnp.int32, (4 * chans, chans), 1)
    member = ((row >> 2) == lane).astype(F32)
    packed = gathered(both, member)
    out_ref[...] = jnp.broadcast_to(packed[None], out_ref.shape)
    for copy in stores:
        copy.wait()


def sums_and_rows(frames, devices):
    count, rows, cols, chans = frames.shape
    pieces = 4
    anywhere = pl.BlockSpec(memory_space=pl.ANY)
    shapes = [(1, rows + 6), (1, rows), (count, 1), (count, 2)]
    return pl.pallas_call(
        functools.partial(sums_kernel, pieces),
        in_specs=[anywhere],
        out_specs=[pl.BlockSpec(memory_space=pltpu.VMEM)] + [anywhere] * 4,
        out_shape=[jax.ShapeDtypeStruct((devices, 2, chans), F32)]
        + [jax.ShapeDtypeStruct(s + (cols, chans), BF16) for s in shapes],
        scratch_shapes=[
            pltpu.VMEM((count, rows, cols, chans), BF16),
            pltpu.SemaphoreType.DMA((count * pieces,)),
            pltpu.SemaphoreType.DMA((10,)),
        ],
        compiler_params=pltpu.CompilerParams(vmem_limit_bytes=60 * 1024 * 1024),
        name="sums_and_rows",
    )(frames)


def block_kernel(
    base, target, groups, scalars, gain_ref, bias_ref, cb_ref, db_ref, sums_ref, w_ref, dw_ref, *rest,
):
    inputs, rest = rest[:groups[0]], rest[groups[0]:]
    out_ref, xin, xs, wa, wbe, wbo, wd, vsum, obuf, sems, osems = rest[:11]
    rows = rest[11:]
    act, res, mix = rows[:19], rows[19:36], rows[36:]
    count, slots = 2, 4
    slab, tile, tiles = scalars[0], scalars[1], scalars[2]

    copies = {}
    used = [0]

    def arrive(step):
        for copy in copies[step]:
            copy.wait()

    def start(step, src, dst):
        copy = pltpu.make_async_copy(src, dst, sems.at[used[0]])
        used[0] += 1
        copy.start()
        copies.setdefault(step, []).append(copy)

    def fetch(step, which, first_row, number, at):
        for slot, n, *places in groups[1]:
            ref, index, row = places[which]
            src = inputs[ref].at[pl.ds(index, n), pl.ds(row + first_row, number)]
            start(step, src, xin.at[pl.ds(slot, n), pl.ds(at, number)])

    fetch(0, 1, 0, 1, 0)
    fetch(0, 0, 0, 3, 1)
    fetch(1, 0, 3, 13, 4)
    fetch(1, 2, 0, 2, 17)

    first = slab * 4 + base
    starts = [jnp.int32(0)] * slots
    ends = [jnp.int32(1)] * slots
    begin = jnp.int32(0)
    for c in range(3, scalars.shape[0]):
        end = begin + scalars[c]
        for f in range(slots):
            inside = (begin <= first + f) & (first + f < end)
            starts[f] = jnp.where(inside, begin, starts[f])
            ends[f] = jnp.where(inside, end, ends[f])
        begin = end
    opens = [starts[f] == first + f for f in range(slots)]
    second = [starts[f] == first + f - 1 for f in range(slots)]

    slabs = sums_ref.shape[0] // 4
    sums = jnp.sum(sums_ref[...].reshape(slabs, 4, 2, 128), axis=1)
    frame_of = 4 * lax.broadcasted_iota(jnp.int32, (slabs, 2, 128), 0) + (
        lax.broadcasted_iota(jnp.int32, (slabs, 2, 128), 2) >> 5
    )
    for f in range(slots):
        inside = (frame_of >= starts[f]) & (frame_of < ends[f])
        vsum[2 * f:2 * f + 2, :] = jnp.sum(jnp.where(inside, sums, 0.0), axis=0)
    group = lax.broadcasted_iota(jnp.int32, (128, 128), 0) & (GROUPS - 1)
    chan = lax.broadcasted_iota(jnp.int32, (128, 128), 1) >> 2
    totals = gathered(vsum[...], (group == chan).astype(F32))
    half_scale, half_shift = [], []
    for f in range(slots):
        pixels = (ends[f] - starts[f]) * (tiles * 16 * 256 * 4)
        number = jnp.full((1, 128), pixels, jnp.int32).astype(F32)
        mean = totals[2 * f:2 * f + 1] / number
        variance = totals[2 * f + 1:2 * f + 2] / number - mean * mean
        scale = gain_ref[...] * lax.rsqrt(variance + EPSILON)
        half_scale.append(0.5 * scale)
        half_shift.append(0.5 * (bias_ref[...] - mean * scale))

    def activate(idx, slot):
        for f in range(slots):
            xs[slot + f] = xin[f, idx].astype(F32)
        for p in range(2):
            lanes = slice(p * 128, (p + 1) * 128)
            planes = []
            for f in range(slots):
                v = xs[slot + f, pl.ds(p, 128, stride=2), :]
                if f >= 2 and 1 <= idx <= 17:
                    res[idx - 1][f - 2, :, lanes] = v.astype(BF16)
                u = v * half_scale[f] + half_shift[f]
                a = u + u * jnp.tanh(u)
                if idx == 0:
                    a = jnp.where(tile == 0, 0.0, a)
                if idx >= 17:
                    a = jnp.where(tile == tiles - 1, 0.0, a)
                planes.append(a.astype(BF16))
            for f in range(2, slots):
                now, before, oldest = planes[f], planes[f - 1], planes[f - 2]
                before = jnp.where(opens[f], now, before)
                oldest = jnp.where(opens[f] | second[f], before, oldest)
                for k, plane in enumerate((oldest, before, now)):
                    act[idx][3 * (f - 2) + k, :, lanes] = plane.astype(BF16)

    def act_step(s):
        rows = [0, 1, 2, 3] if s == 0 else ([2 * s + 2, 2 * s + 3] if s < 8 else [18])
        for i, idx in enumerate(rows):
            activate(idx, (s % 2) * 4 * slots + i * slots)

    def build_weights():
        zero = jnp.zeros((128, 128), BF16)
        for k in range(3):
            for dy in range(3):
                w0, w1, w2 = (w_ref[k, dy, dx] for dx in range(3))
                r = (dy * 3 + k) * 256
                wa[r:r + 128, 0:128] = w1
                wa[r:r + 128, 128:256] = w0
                wa[r + 128:r + 256, 0:128] = w2
                wa[r + 128:r + 256, 128:256] = w1
                for wb, w in ((wbe, w0), (wbo, w2)):
                    a = (dy * 3 + k) * 128
                    b = ((dy + 1) * 3 + k) * 128
                    wb[a:a + 128, 0:128] = w
                    wb[b:b + 128, 128:256] = w
            for wb in (wbe, wbo):
                wb[k * 128:(k + 1) * 128, 128:256] = zero
                wb[(9 + k) * 128:(10 + k) * 128, 0:128] = zero
        for dy in range(3):
            r = dy * 256
            wd[r:r + 128, 0:128] = dw_ref[dy, 0]
            wd[r + 128:r + 256, 0:128] = dw_ref[dy, 1]
            wd[r:r + 128, 128:256] = dw_ref[dy, 2]
            wd[r + 128:r + 256, 128:256] = zero

    pair = lax.broadcasted_iota(jnp.int32, (128, 128), 0)

    def from_before(p):
        return jnp.where(pair == 0, 0.0, pltpu.roll(p, 1, 0))

    def from_after(p):
        return jnp.where(pair == 127, 0.0, pltpu.roll(p, 127, 0))

    cb = jnp.concatenate([cb_ref[...], cb_ref[...]], axis=1)

    def dot(a, b):
        return jnp.dot(a, b, preferred_element_type=F32)

    def finish(y, t, own, even, odd):
        m = res[y][t].astype(F32) + cb + own
        for p, v in ((0, m[:, :128] + from_before(even)), (1, m[:, 128:] + from_after(odd))):
            if y == 16:
                v = jnp.where(tile == tiles - 1, 0.0, v)
            mix[y][t, :, p * 128:(p + 1) * 128] = v.astype(BF16)

    def conv_step(s):
        y = 2 * s
        n = 1 if s == 8 else 2
        for t in range(count):
            blocks = [
                jnp.concatenate([act[y + i + dy][3 * t + k] for dy in range(3) for k in range(3)], axis=1)
                for i in range(n)
            ]
            own = dot(jnp.concatenate(blocks, axis=0), wa[...])
            sides = []
            for p, wb in ((1, wbe), (0, wbo)):
                left = jnp.concatenate(
                    [act[y + q][3 * t + k, :, p * 128:(p + 1) * 128] for q in range(n + 2) for k in range(3)],
                    axis=1)
                sides.append(dot(left, wb[...] if n == 2 else wb[0:1152, 0:128]))
            for i in range(n):
                even, odd = (v[:, i * 128:(i + 1) * 128] for v in sides)
                finish(y + i, t, own[i * 128:(i + 1) * 128], even, odd)

    def out_row(r):
        left = jnp.concatenate(
            [jnp.concatenate([mix[2 * r + dy][t] for dy in range(3)], axis=1) for t in range(count)], axis=0)
        p = dot(left, wd[...])
        for t in range(count):
            q = p[t * 128:(t + 1) * 128]
            obuf[t, r] = (q[:, :128] + from_after(q[:, 128:]) + db_ref[...]).astype(BF16)

    leaving = []

    def leave(first_row, number):
        cut = pl.ds(first_row, number)
        copy = pltpu.make_async_copy(obuf.at[:, cut], out_ref.at[pl.ds(target, 2), cut], osems.at[len(leaving)])
        copy.start()
        leaving.append(copy)

    build_weights()
    arrive(0)
    act_step(0)
    for s in range(9):
        conv_step(s)
        if s == 0:
            arrive(1)
        if s < 8:
            act_step(s + 1)
        if s >= 2:
            out_row(s - 2)
    leave(0, 7)
    out_row(7)
    leave(7, 1)
    for copy in leaving:
        copy.wait()


def two_frames(base, target, scalars, vectors, shared, big, groups, flops, unread):
    anywhere = pl.BlockSpec(memory_space=pl.ANY)
    smem = pl.BlockSpec(memory_space=pltpu.SMEM)
    out = jax.ShapeDtypeStruct((4, 8, 128, 128), BF16)
    scratch = [
        pltpu.VMEM((4, 19, 256, 128), BF16),
        pltpu.VMEM((32, 256, 128), F32),
        pltpu.VMEM((2304, 256), BF16),
        pltpu.VMEM((1536, 256), BF16),
        pltpu.VMEM((1536, 256), BF16),
        pltpu.VMEM((768, 256), BF16),
        pltpu.VMEM((8, 128), F32),
        pltpu.VMEM((2, 8, 128, 128), BF16),
        pltpu.SemaphoreType.DMA((4 * len(groups),)),
        pltpu.SemaphoreType.DMA((2,)),
    ]
    scratch += [pltpu.VMEM((6, 128, 256), BF16)] * 19
    scratch += [pltpu.VMEM((2, 128, 256), BF16)] * 34
    operands = [scalars, *vectors, *shared, *big, *unread]
    near_by = len(vectors) + len(shared)
    specs = [smem] + [pl.BlockSpec(memory_space=pltpu.VMEM)] * near_by + [anywhere] * (len(big) + len(unread))
    return pl.pallas_call(
        functools.partial(block_kernel, base, target, (len(big) + len(unread), groups)),
        out_shape=out,
        in_specs=specs,
        out_specs=anywhere,
        scratch_shapes=scratch,
        input_output_aliases={len(operands) - 1: 0} if target == 0 else {},
        compiler_params=pltpu.CompilerParams(vmem_limit_bytes=VMEM_LIMIT),
        cost_estimate=pl.CostEstimate(flops=flops, bytes_accessed=6 * 2**20, transcendentals=10**7),
        name="two_frames",
    )(*operands)


def shards(frames, clip_frames, norm_gain, norm_bias, conv_weight, conv_bias, down_weight, down_bias):
    slabs, tiles = lax.axis_size("slab"), lax.axis_size("tile")
    both = ("slab", "tile")

    frames = pltpu.with_memory_space_constraint(frames, pltpu.HBM)
    sums, far, near, top, bottom = sums_and_rows(frames, slabs * tiles)
    sums = lax.all_to_all(sums, both, 0, 0)
    top = lax.ppermute(top, "tile", [(t, t + 1) for t in range(tiles - 1)])
    bottom = lax.ppermute(bottom, "tile", [(t + 1, t) for t in range(tiles - 1)])
    along = [(s, s + 1) for s in range(slabs - 1)]
    near = lax.ppermute(near, "slab", along)
    corners = [top[2:4].reshape(1, 2, *top.shape[2:]), bottom[2:4].reshape(1, 4, *bottom.shape[2:])]
    far = lax.dynamic_update_slice(far, jnp.concatenate(corners, axis=1), (0, 16, 0, 0))
    far = lax.ppermute(far, "slab", along)
    place = jnp.stack([lax.axis_index("slab"), lax.axis_index("tile"), jnp.int32(tiles)]).astype(jnp.int32)
    scalars, shared = jnp.concatenate([place, clip_frames]), (sums, conv_weight, down_weight)
    vectors = [v[None] for v in (norm_gain, norm_bias, conv_bias, down_bias)]
    last = two_frames(
        0, 2, scalars, vectors, shared, (frames, top, bottom), [(0, 4, (0, 0, 0), (1, 0, 0), (2, 0, 0))], FLOPS, (near,))
    groups = [
        (0, 1, (0, 0, 0), (0, 0, 16), (0, 0, 18)),
        (1, 1, (1, 0, 0), (0, 0, 17), (0, 0, 20)),
        (2, 2, (2, 0, 0), (3, 0, 0), (4, 0, 0)),
    ]
    return two_frames(-2, 0, scalars, vectors, shared, (far, near, frames, top, bottom), groups, FLOPS, (last,))


def solution(mesh):
    return jax.shard_map(
        shards,
        mesh=mesh,
        in_specs=(P("slab", "tile", None, None), P(), P(), P(), P(), P(), P(), P()),
        out_specs=P("slab", "tile", None, None),
        check_vma=False,
    )
```

```python
import functools

import jax
import jax.numpy as jnp
from jax import lax
from jax.experimental import pallas as pl
from jax.experimental.pallas import tpu as pltpu
from jax.sharding import PartitionSpec as P

GROUPS = 32
EPSILON = 1e-06
VMEM_LIMIT = 36 * 1024 * 1024
FLOPS = 200 * 10**9
F32 = jnp.float32
BF16 = jnp.bfloat16


def gathered(x, member):
    parts = []
    for _ in range(3):
        parts.append(x.astype(BF16))
        x = x - parts[-1].astype(F32)
    n = x.shape[0]
    out = jnp.dot(jnp.concatenate(parts, axis=0), member.astype(BF16), preferred_element_type=F32)
    return out[:n] + out[n:2 * n] + out[2 * n:]


def sums_kernel(pieces, x_ref, out_ref, far_ref, near_ref, top_ref, bottom_ref, xin, load, store):
    count, rows, cols, chans = x_ref.shape
    part = rows // pieces
    order = [2, 3, 0, 1]
    loads = {}
    for f in order:
        for p in range(pieces):
            cut = pl.ds(p * part, part)
            copy = pltpu.make_async_copy(x_ref.at[f, cut], xin.at[f, cut], load.at[f * pieces + p])
            copy.start()
            loads[f, p] = copy
    stores = []

    def send(src, dst):
        copy = pltpu.make_async_copy(src, dst, store.at[len(stores)])
        copy.start()
        stores.append(copy)

    sums = {}
    for f in order:
        one = two = jnp.zeros((32, chans), F32)
        for p in range(pieces):
            loads[f, p].wait()
            if p == pieces - 1:
                send(xin.at[f, pl.ds(0, 2)], bottom_ref.at[f])
                send(xin.at[f, pl.ds(rows - 1, 1)], top_ref.at[f])
                if f >= 2:
                    send(xin.at[f], (far_ref.at[0, pl.ds(0, rows)], near_ref.at[0])[f - 2])

            def row(i, both, f=f, p=p):
                x = xin[f, p * part + i].astype(F32).reshape(cols // 32, 32, chans)
                return both[0] + jnp.sum(x, axis=0), both[1] + jnp.sum(x * x, axis=0)

            one, two = lax.fori_loop(0, part, row, (one, two))
        sums[f] = [jnp.sum(v, axis=0, keepdims=True) for v in (one, two)]
    both = jnp.concatenate([jnp.concatenate([sums[f][i] for f in range(count)], axis=1) for i in range(2)], axis=0)
    row = lax.broadcasted_iota(jnp.int32, (4 * chans, chans), 0)
    lane = lax.broadcasted_iota(jnp.int32, (4 * chans, chans), 1)
    member = ((row >> 2) == lane).astype(F32)
    packed = gathered(both, member)
    out_ref[...] = jnp.broadcast_to(packed[None], out_ref.shape)
    for copy in stores:
        copy.wait()


def sums_and_rows(frames, devices):
    count, rows, cols, chans = frames.shape
    pieces = 4
    anywhere = pl.BlockSpec(memory_space=pl.ANY)
    shapes = [(1, rows + 6), (1, rows), (count, 1), (count, 2)]
    return pl.pallas_call(
        functools.partial(sums_kernel, pieces),
        in_specs=[anywhere],
        out_specs=[pl.BlockSpec(memory_space=pltpu.VMEM)] + [anywhere] * 4,
        out_shape=[jax.ShapeDtypeStruct((devices, 2, chans), F32)]
        + [jax.ShapeDtypeStruct(s + (cols, chans), BF16) for s in shapes],
        scratch_shapes=[
            pltpu.VMEM((count, rows, cols, chans), BF16),
            pltpu.SemaphoreType.DMA((count * pieces,)),
            pltpu.SemaphoreType.DMA((10,)),
        ],
        compiler_params=pltpu.CompilerParams(vmem_limit_bytes=60 * 1024 * 1024),
        name="sums_and_rows",
    )(frames)


def block_kernel(
    base, target, groups, scalars, gain_ref, bias_ref, cb_ref, db_ref, sums_ref, w_ref, dw_ref, *rest,
):
    inputs, rest = rest[:groups[0]], rest[groups[0]:]
    out_ref, xin, xs, wa, wbe, wbo, wd, vsum, obuf, sems, osems = rest[:11]
    rows = rest[11:]
    act, res, mix = rows[:19], rows[19:36], rows[36:]
    count, slots = 2, 4
    slab, tile, tiles = scalars[0], scalars[1], scalars[2]

    copies = {}
    used = [0]

    def arrive(step):
        for copy in copies[step]:
            copy.wait()

    def start(step, src, dst):
        copy = pltpu.make_async_copy(src, dst, sems.at[used[0]])
        used[0] += 1
        copy.start()
        copies.setdefault(step, []).append(copy)

    def fetch(step, which, first_row, number, at):
        for slot, n, *places in groups[1]:
            ref, index, row = places[which]
            src = inputs[ref].at[pl.ds(index, n), pl.ds(row + first_row, number)]
            start(step, src, xin.at[pl.ds(slot, n), pl.ds(at, number)])

    fetch(0, 1, 0, 1, 0)
    fetch(0, 0, 0, 3, 1)
    fetch(1, 0, 3, 13, 4)
    fetch(1, 2, 0, 2, 17)

    first = slab * 4 + base
    starts = [jnp.int32(0)] * slots
    ends = [jnp.int32(1)] * slots
    begin = jnp.int32(0)
    for c in range(3, scalars.shape[0]):
        end = begin + scalars[c]
        for f in range(slots):
            inside = (begin <= first + f) & (first + f < end)
            starts[f] = jnp.where(inside, begin, starts[f])
            ends[f] = jnp.where(inside, end, ends[f])
        begin = end
    opens = [starts[f] == first + f for f in range(slots)]
    second = [starts[f] == first + f - 1 for f in range(slots)]

    slabs = sums_ref.shape[0] // 4
    sums = jnp.sum(sums_ref[...].reshape(slabs, 4, 2, 128), axis=1)
    frame_of = 4 * lax.broadcasted_iota(jnp.int32, (slabs, 2, 128), 0) + (
        lax.broadcasted_iota(jnp.int32, (slabs, 2, 128), 2) >> 5
    )
    for f in range(slots):
        inside = (frame_of >= starts[f]) & (frame_of < ends[f])
        vsum[2 * f:2 * f + 2, :] = jnp.sum(jnp.where(inside, sums, 0.0), axis=0)
    group = lax.broadcasted_iota(jnp.int32, (128, 128), 0) & (GROUPS - 1)
    chan = lax.broadcasted_iota(jnp.int32, (128, 128), 1) >> 2
    totals = gathered(vsum[...], (group == chan).astype(F32))
    half_scale, half_shift = [], []
    for f in range(slots):
        pixels = (ends[f] - starts[f]) * (tiles * 16 * 256 * 4)
        number = jnp.full((1, 128), pixels, jnp.int32).astype(F32)
        mean = totals[2 * f:2 * f + 1] / number
        variance = totals[2 * f + 1:2 * f + 2] / number - mean * mean
        scale = gain_ref[...] * lax.rsqrt(variance + EPSILON)
        half_scale.append(0.5 * scale)
        half_shift.append(0.5 * (bias_ref[...] - mean * scale))

    def activate(idx, slot):
        for f in range(slots):
            xs[slot + f] = xin[f, idx].astype(F32)
        for p in range(2):
            lanes = slice(p * 128, (p + 1) * 128)
            planes = []
            for f in range(slots):
                v = xs[slot + f, pl.ds(p, 128, stride=2), :]
                if f >= 2 and 1 <= idx <= 17:
                    res[idx - 1][f - 2, :, lanes] = v.astype(BF16)
                u = v * half_scale[f] + half_shift[f]
                a = u + u * jnp.tanh(u)
                if idx == 0:
                    a = jnp.where(tile == 0, 0.0, a)
                if idx >= 17:
                    a = jnp.where(tile == tiles - 1, 0.0, a)
                planes.append(a.astype(BF16))
            for f in range(2, slots):
                now, before, oldest = planes[f], planes[f - 1], planes[f - 2]
                before = jnp.where(opens[f], now, before)
                oldest = jnp.where(opens[f] | second[f], before, oldest)
                for k, plane in enumerate((oldest, before, now)):
                    act[idx][3 * (f - 2) + k, :, lanes] = plane.astype(BF16)

    def act_step(s):
        rows = [0, 1, 2, 3] if s == 0 else ([2 * s + 2, 2 * s + 3] if s < 8 else [18])
        for i, idx in enumerate(rows):
            activate(idx, (s % 2) * 4 * slots + i * slots)

    def build_weights():
        zero = jnp.zeros((128, 128), BF16)
        for k in range(3):
            for dy in range(3):
                w0, w1, w2 = (w_ref[k, dy, dx] for dx in range(3))
                r = (dy * 3 + k) * 256
                wa[r:r + 128, 0:128] = w1
                wa[r:r + 128, 128:256] = w0
                wa[r + 128:r + 256, 0:128] = w2
                wa[r + 128:r + 256, 128:256] = w1
                for wb, w in ((wbe, w0), (wbo, w2)):
                    a = (dy * 3 + k) * 128
                    b = ((dy + 1) * 3 + k) * 128
                    wb[a:a + 128, 0:128] = w
                    wb[b:b + 128, 128:256] = w
            for wb in (wbe, wbo):
                wb[k * 128:(k + 1) * 128, 128:256] = zero
                wb[(9 + k) * 128:(10 + k) * 128, 0:128] = zero
        for dy in range(3):
            r = dy * 256
            wd[r:r + 128, 0:128] = dw_ref[dy, 0]
            wd[r + 128:r + 256, 0:128] = dw_ref[dy, 1]
            wd[r:r + 128, 128:256] = dw_ref[dy, 2]
            wd[r + 128:r + 256, 128:256] = zero

    pair = lax.broadcasted_iota(jnp.int32, (128, 128), 0)

    def from_before(p):
        return jnp.where(pair == 0, 0.0, pltpu.roll(p, 1, 0))

    def from_after(p):
        return jnp.where(pair == 127, 0.0, pltpu.roll(p, 127, 0))

    cb = jnp.concatenate([cb_ref[...], cb_ref[...]], axis=1)

    def dot(a, b):
        return jnp.dot(a, b, preferred_element_type=F32)

    def finish(y, t, own, even, odd):
        m = res[y][t].astype(F32) + cb + own
        for p, v in ((0, m[:, :128] + from_before(even)), (1, m[:, 128:] + from_after(odd))):
            if y == 16:
                v = jnp.where(tile == tiles - 1, 0.0, v)
            mix[y][t, :, p * 128:(p + 1) * 128] = v.astype(BF16)

    def conv_step(s):
        y = 2 * s
        n = 1 if s == 8 else 2
        for t in range(count):
            blocks = [
                jnp.concatenate([act[y + i + dy][3 * t + k] for dy in range(3) for k in range(3)], axis=1)
                for i in range(n)
            ]
            own = dot(jnp.concatenate(blocks, axis=0), wa[...])
            sides = []
            for p, wb in ((1, wbe), (0, wbo)):
                left = jnp.concatenate(
                    [act[y + q][3 * t + k, :, p * 128:(p + 1) * 128] for q in range(n + 2) for k in range(3)],
                    axis=1)
                sides.append(dot(left, wb[...] if n == 2 else wb[0:1152, 0:128]))
            for i in range(n):
                even, odd = (v[:, i * 128:(i + 1) * 128] for v in sides)
                finish(y + i, t, own[i * 128:(i + 1) * 128], even, odd)

    def out_row(r):
        left = jnp.concatenate(
            [jnp.concatenate([mix[2 * r + dy][t] for dy in range(3)], axis=1) for t in range(count)], axis=0)
        p = dot(left, wd[...])
        for t in range(count):
            q = p[t * 128:(t + 1) * 128]
            obuf[t, r] = (q[:, :128] + from_after(q[:, 128:]) + db_ref[...]).astype(BF16)

    leaving = []

    def leave(first_row, number):
        cut = pl.ds(first_row, number)
        copy = pltpu.make_async_copy(obuf.at[:, cut], out_ref.at[pl.ds(target, 2), cut], osems.at[len(leaving)])
        copy.start()
        leaving.append(copy)

    build_weights()
    arrive(0)
    act_step(0)
    for s in range(9):
        conv_step(s)
        if s == 0:
            arrive(1)
        if s < 8:
            act_step(s + 1)
    for r in range(8):
        out_row(r)
        if r == 5:
            leave(0, 6)
    leave(6, 2)
    for copy in leaving:
        copy.wait()


def two_frames(base, target, scalars, vectors, shared, big, groups, flops, unread):
    anywhere = pl.BlockSpec(memory_space=pl.ANY)
    smem = pl.BlockSpec(memory_space=pltpu.SMEM)
    out = jax.ShapeDtypeStruct((4, 8, 128, 128), BF16)
    scratch = [
        pltpu.VMEM((4, 19, 256, 128), BF16),
        pltpu.VMEM((32, 256, 128), F32),
        pltpu.VMEM((2304, 256), BF16),
        pltpu.VMEM((1536, 256), BF16),
        pltpu.VMEM((1536, 256), BF16),
        pltpu.VMEM((768, 256), BF16),
        pltpu.VMEM((8, 128), F32),
        pltpu.VMEM((2, 8, 128, 128), BF16),
        pltpu.SemaphoreType.DMA((4 * len(groups),)),
        pltpu.SemaphoreType.DMA((2,)),
    ]
    scratch += [pltpu.VMEM((6, 128, 256), BF16)] * 19
    scratch += [pltpu.VMEM((2, 128, 256), BF16)] * 34
    operands = [scalars, *vectors, *shared, *big, *unread]
    near_by = len(vectors) + len(shared)
    specs = [smem] + [pl.BlockSpec(memory_space=pltpu.VMEM)] * near_by + [anywhere] * (len(big) + len(unread))
    return pl.pallas_call(
        functools.partial(block_kernel, base, target, (len(big) + len(unread), groups)),
        out_shape=out,
        in_specs=specs,
        out_specs=anywhere,
        scratch_shapes=scratch,
        input_output_aliases={len(operands) - 1: 0} if target == 0 else {},
        compiler_params=pltpu.CompilerParams(vmem_limit_bytes=VMEM_LIMIT),
        cost_estimate=pl.CostEstimate(flops=flops, bytes_accessed=6 * 2**20, transcendentals=10**7),
        name="two_frames",
    )(*operands)


def shards(frames, clip_frames, norm_gain, norm_bias, conv_weight, conv_bias, down_weight, down_bias):
    slabs, tiles = lax.axis_size("slab"), lax.axis_size("tile")
    both = ("slab", "tile")

    frames = pltpu.with_memory_space_constraint(frames, pltpu.HBM)
    sums, far, near, top, bottom = sums_and_rows(frames, slabs * tiles)
    sums = lax.all_to_all(sums, both, 0, 0)
    top = lax.ppermute(top, "tile", [(t, t + 1) for t in range(tiles - 1)])
    bottom = lax.ppermute(bottom, "tile", [(t + 1, t) for t in range(tiles - 1)])
    along = [(s, s + 1) for s in range(slabs - 1)]
    near = lax.ppermute(near, "slab", along)
    corners = [top[2:4].reshape(1, 2, *top.shape[2:]), bottom[2:4].reshape(1, 4, *bottom.shape[2:])]
    far = lax.dynamic_update_slice(far, jnp.concatenate(corners, axis=1), (0, 16, 0, 0))
    far = lax.ppermute(far, "slab", along)
    place = jnp.stack([lax.axis_index("slab"), lax.axis_index("tile"), jnp.int32(tiles)]).astype(jnp.int32)
    scalars, shared = jnp.concatenate([place, clip_frames]), (sums, conv_weight, down_weight)
    vectors = [v[None] for v in (norm_gain, norm_bias, conv_bias, down_bias)]
    last = two_frames(
        0, 2, scalars, vectors, shared, (frames, top, bottom), [(0, 4, (0, 0, 0), (1, 0, 0), (2, 0, 0))], FLOPS, (near,))
    groups = [
        (0, 1, (0, 0, 0), (0, 0, 16), (0, 0, 18)),
        (1, 1, (1, 0, 0), (0, 0, 17), (0, 0, 20)),
        (2, 2, (2, 0, 0), (3, 0, 0), (4, 0, 0)),
    ]
    return two_frames(-2, 0, scalars, vectors, shared, (far, near, frames, top, bottom), groups, FLOPS, (last,))


def solution(mesh):
    return jax.shard_map(
        shards,
        mesh=mesh,
        in_specs=(P("slab", "tile", None, None), P(), P(), P(), P(), P(), P(), P()),
        out_specs=P("slab", "tile", None, None),
        check_vma=False,
    )
```

```python
import functools

import jax
import jax.numpy as jnp
from jax import lax
from jax.experimental import pallas as pl
from jax.experimental.pallas import tpu as pltpu
from jax.sharding import PartitionSpec as P

GROUPS = 32
EPSILON = 1e-06
VMEM_LIMIT = 36 * 1024 * 1024
FLOPS = 200 * 10**9
F32 = jnp.float32
BF16 = jnp.bfloat16


def gathered(x, member):
    parts = []
    for _ in range(3):
        parts.append(x.astype(BF16))
        x = x - parts[-1].astype(F32)
    n = x.shape[0]
    out = jnp.dot(jnp.concatenate(parts, axis=0), member.astype(BF16), preferred_element_type=F32)
    return out[:n] + out[n:2 * n] + out[2 * n:]


def sums_kernel(pieces, x_ref, out_ref, far_ref, near_ref, top_ref, bottom_ref, xin, load, store):
    count, rows, cols, chans = x_ref.shape
    part = rows // pieces
    order = [2, 3, 0, 1]
    loads = {}
    for f in order:
        for p in range(pieces):
            cut = pl.ds(p * part, part)
            copy = pltpu.make_async_copy(x_ref.at[f, cut], xin.at[f, cut], load.at[f * pieces + p])
            copy.start()
            loads[f, p] = copy
    stores = []

    def send(src, dst):
        copy = pltpu.make_async_copy(src, dst, store.at[len(stores)])
        copy.start()
        stores.append(copy)

    sums = {}
    for f in order:
        one = two = jnp.zeros((32, chans), F32)
        for p in range(pieces):
            loads[f, p].wait()
            if p == pieces - 1:
                send(xin.at[f, pl.ds(0, 2)], bottom_ref.at[f])
                send(xin.at[f, pl.ds(rows - 1, 1)], top_ref.at[f])
                if f >= 2:
                    send(xin.at[f], (far_ref.at[0, pl.ds(0, rows)], near_ref.at[0])[f - 2])

            def row(i, both, f=f, p=p):
                x = xin[f, p * part + i].astype(F32).reshape(cols // 32, 32, chans)
                return both[0] + jnp.sum(x, axis=0), both[1] + jnp.sum(x * x, axis=0)

            one, two = lax.fori_loop(0, part, row, (one, two))
        sums[f] = [jnp.sum(v, axis=0, keepdims=True) for v in (one, two)]
    both = jnp.concatenate([jnp.concatenate([sums[f][i] for f in range(count)], axis=1) for i in range(2)], axis=0)
    row = lax.broadcasted_iota(jnp.int32, (4 * chans, chans), 0)
    lane = lax.broadcasted_iota(jnp.int32, (4 * chans, chans), 1)
    member = ((row >> 2) == lane).astype(F32)
    packed = gathered(both, member)
    out_ref[...] = jnp.broadcast_to(packed[None], out_ref.shape)
    for copy in stores:
        copy.wait()


def sums_and_rows(frames, devices):
    count, rows, cols, chans = frames.shape
    pieces = 4
    anywhere = pl.BlockSpec(memory_space=pl.ANY)
    shapes = [(1, rows + 6), (1, rows), (count, 1), (count, 2)]
    return pl.pallas_call(
        functools.partial(sums_kernel, pieces),
        in_specs=[anywhere],
        out_specs=[pl.BlockSpec(memory_space=pltpu.VMEM)] + [anywhere] * 4,
        out_shape=[jax.ShapeDtypeStruct((devices, 2, chans), F32)]
        + [jax.ShapeDtypeStruct(s + (cols, chans), BF16) for s in shapes],
        scratch_shapes=[
            pltpu.VMEM((count, rows, cols, chans), BF16),
            pltpu.SemaphoreType.DMA((count * pieces,)),
            pltpu.SemaphoreType.DMA((10,)),
        ],
        compiler_params=pltpu.CompilerParams(vmem_limit_bytes=60 * 1024 * 1024),
        name="sums_and_rows",
    )(frames)


def block_kernel(
    base, target, groups, scalars, gain_ref, bias_ref, cb_ref, db_ref, sums_ref, w_ref, dw_ref, *rest,
):
    inputs, rest = rest[:groups[0]], rest[groups[0]:]
    out_ref, xin, xs, wa, wbe, wbo, wd, vsum, obuf, sems, osems = rest[:11]
    rows = rest[11:]
    act, res, mix = rows[:19], rows[19:36], rows[36:]
    count, slots = 2, 4
    slab, tile, tiles = scalars[0], scalars[1], scalars[2]

    copies = {}
    used = [0]

    def arrive(step):
        for copy in copies[step]:
            copy.wait()

    def start(step, src, dst):
        copy = pltpu.make_async_copy(src, dst, sems.at[used[0]])
        used[0] += 1
        copy.start()
        copies.setdefault(step, []).append(copy)

    def fetch(step, which, first_row, number, at):
        for slot, n, *places in groups[1]:
            ref, index, row = places[which]
            src = inputs[ref].at[pl.ds(index, n), pl.ds(row + first_row, number)]
            start(step, src, xin.at[pl.ds(slot, n), pl.ds(at, number)])

    fetch(0, 1, 0, 1, 0)
    fetch(0, 0, 0, 3, 1)
    fetch(1, 0, 3, 13, 4)
    fetch(1, 2, 0, 2, 17)

    first = slab * 4 + base
    starts = [jnp.int32(0)] * slots
    ends = [jnp.int32(1)] * slots
    begin = jnp.int32(0)
    for c in range(3, scalars.shape[0]):
        end = begin + scalars[c]
        for f in range(slots):
            inside = (begin <= first + f) & (first + f < end)
            starts[f] = jnp.where(inside, begin, starts[f])
            ends[f] = jnp.where(inside, end, ends[f])
        begin = end
    opens = [starts[f] == first + f for f in range(slots)]
    second = [starts[f] == first + f - 1 for f in range(slots)]

    slabs = sums_ref.shape[0] // 4
    sums = jnp.sum(sums_ref[...].reshape(slabs, 4, 2, 128), axis=1)
    frame_of = 4 * lax.broadcasted_iota(jnp.int32, (slabs, 2, 128), 0) + (
        lax.broadcasted_iota(jnp.int32, (slabs, 2, 128), 2) >> 5
    )
    for f in range(slots):
        inside = (frame_of >= starts[f]) & (frame_of < ends[f])
        vsum[2 * f:2 * f + 2, :] = jnp.sum(jnp.where(inside, sums, 0.0), axis=0)
    group = lax.broadcasted_iota(jnp.int32, (128, 128), 0) & (GROUPS - 1)
    chan = lax.broadcasted_iota(jnp.int32, (128, 128), 1) >> 2
    totals = gathered(vsum[...], (group == chan).astype(F32))
    half_scale, half_shift = [], []
    for f in range(slots):
        pixels = (ends[f] - starts[f]) * (tiles * 16 * 256 * 4)
        number = jnp.full((1, 128), pixels, jnp.int32).astype(F32)
        mean = totals[2 * f:2 * f + 1] / number
        variance = totals[2 * f + 1:2 * f + 2] / number - mean * mean
        scale = gain_ref[...] * lax.rsqrt(variance + EPSILON)
        half_scale.append(0.5 * scale)
        half_shift.append(0.5 * (bias_ref[...] - mean * scale))

    def activate(idx, slot):
        for f in range(slots):
            xs[slot + f] = xin[f, idx].astype(F32)
        for p in range(2):
            lanes = slice(p * 128, (p + 1) * 128)
            planes = []
            for f in range(slots):
                v = xs[slot + f, pl.ds(p, 128, stride=2), :]
                if f >= 2 and 1 <= idx <= 17:
                    res[idx - 1][f - 2, :, lanes] = v.astype(BF16)
                u = v * half_scale[f] + half_shift[f]
                a = u + u * jnp.tanh(u)
                if idx == 0:
                    a = jnp.where(tile == 0, 0.0, a)
                if idx >= 17:
                    a = jnp.where(tile == tiles - 1, 0.0, a)
                planes.append(a.astype(BF16))
            for f in range(2, slots):
                now, before, oldest = planes[f], planes[f - 1], planes[f - 2]
                before = jnp.where(opens[f], now, before)
                oldest = jnp.where(opens[f] | second[f], before, oldest)
                for k, plane in enumerate((oldest, before, now)):
                    act[idx][3 * (f - 2) + k, :, lanes] = plane.astype(BF16)

    def act_step(s):
        rows = [0, 1, 2, 3] if s == 0 else ([2 * s + 2, 2 * s + 3] if s < 8 else [18])
        for i, idx in enumerate(rows):
            activate(idx, (s % 2) * 4 * slots + i * slots)

    def build_weights():
        zero = jnp.zeros((128, 128), BF16)
        for k in range(3):
            for dy in range(3):
                w0, w1, w2 = (w_ref[k, dy, dx] for dx in range(3))
                r = (dy * 3 + k) * 256
                wa[r:r + 128, 0:128] = w1
                wa[r:r + 128, 128:256] = w0
                wa[r + 128:r + 256, 0:128] = w2
                wa[r + 128:r + 256, 128:256] = w1
                for wb, w in ((wbe, w0), (wbo, w2)):
                    a = (dy * 3 + k) * 128
                    b = ((dy + 1) * 3 + k) * 128
                    wb[a:a + 128, 0:128] = w
                    wb[b:b + 128, 128:256] = w
            for wb in (wbe, wbo):
                wb[k * 128:(k + 1) * 128, 128:256] = zero
                wb[(9 + k) * 128:(10 + k) * 128, 0:128] = zero
        for dy in range(3):
            r = dy * 256
            wd[r:r + 128, 0:128] = dw_ref[dy, 0]
            wd[r + 128:r + 256, 0:128] = dw_ref[dy, 1]
            wd[r:r + 128, 128:256] = dw_ref[dy, 2]
            wd[r + 128:r + 256, 128:256] = zero

    pair = lax.broadcasted_iota(jnp.int32, (128, 128), 0)

    def from_before(p):
        return jnp.where(pair == 0, 0.0, pltpu.roll(p, 1, 0))

    def from_after(p):
        return jnp.where(pair == 127, 0.0, pltpu.roll(p, 127, 0))

    cb = jnp.concatenate([cb_ref[...], cb_ref[...]], axis=1)

    def dot(a, b):
        return jnp.dot(a, b, preferred_element_type=F32)

    def finish(y, t, own, even, odd):
        m = res[y][t].astype(F32) + cb + own
        for p, v in ((0, m[:, :128] + from_before(even)), (1, m[:, 128:] + from_after(odd))):
            if y == 16:
                v = jnp.where(tile == tiles - 1, 0.0, v)
            mix[y][t, :, p * 128:(p + 1) * 128] = v.astype(BF16)

    def conv_step(s):
        y = 2 * s
        n = 1 if s == 8 else 2
        for t in range(count):
            blocks = [
                jnp.concatenate([act[y + i + dy][3 * t + k] for dy in range(3) for k in range(3)], axis=1)
                for i in range(n)
            ]
            own = dot(jnp.concatenate(blocks, axis=0), wa[...])
            sides = []
            for p, wb in ((1, wbe), (0, wbo)):
                left = jnp.concatenate(
                    [act[y + q][3 * t + k, :, p * 128:(p + 1) * 128] for q in range(n + 2) for k in range(3)],
                    axis=1)
                sides.append(dot(left, wb[...] if n == 2 else wb[0:1152, 0:128]))
            for i in range(n):
                even, odd = (v[:, i * 128:(i + 1) * 128] for v in sides)
                finish(y + i, t, own[i * 128:(i + 1) * 128], even, odd)

    def out_row(r):
        left = jnp.concatenate(
            [jnp.concatenate([mix[2 * r + dy][t] for dy in range(3)], axis=1) for t in range(count)], axis=0)
        p = dot(left, wd[...])
        for t in range(count):
            q = p[t * 128:(t + 1) * 128]
            obuf[t, r] = (q[:, :128] + from_after(q[:, 128:]) + db_ref[...]).astype(BF16)

    leaving = []

    def leave(first_row, number):
        cut = pl.ds(first_row, number)
        copy = pltpu.make_async_copy(obuf.at[:, cut], out_ref.at[pl.ds(target, 2), cut], osems.at[len(leaving)])
        copy.start()
        leaving.append(copy)

    build_weights()
    arrive(0)
    act_step(0)
    arrive(1)
    for s in range(9):
        conv_step(s)
        if s < 8:
            act_step(s + 1)
    for r in range(8):
        out_row(r)
        if r == 5:
            leave(0, 6)
    leave(6, 2)
    for copy in leaving:
        copy.wait()


def two_frames(base, target, scalars, vectors, shared, big, groups, flops, unread):
    anywhere = pl.BlockSpec(memory_space=pl.ANY)
    smem = pl.BlockSpec(memory_space=pltpu.SMEM)
    out = jax.ShapeDtypeStruct((4, 8, 128, 128), BF16)
    scratch = [
        pltpu.VMEM((4, 19, 256, 128), BF16),
        pltpu.VMEM((32, 256, 128), F32),
        pltpu.VMEM((2304, 256), BF16),
        pltpu.VMEM((1536, 256), BF16),
        pltpu.VMEM((1536, 256), BF16),
        pltpu.VMEM((768, 256), BF16),
        pltpu.VMEM((8, 128), F32),
        pltpu.VMEM((2, 8, 128, 128), BF16),
        pltpu.SemaphoreType.DMA((4 * len(groups),)),
        pltpu.SemaphoreType.DMA((2,)),
    ]
    scratch += [pltpu.VMEM((6, 128, 256), BF16)] * 19
    scratch += [pltpu.VMEM((2, 128, 256), BF16)] * 34
    operands = [scalars, *vectors, *shared, *big, *unread]
    near_by = len(vectors) + len(shared)
    specs = [smem] + [pl.BlockSpec(memory_space=pltpu.VMEM)] * near_by + [anywhere] * (len(big) + len(unread))
    return pl.pallas_call(
        functools.partial(block_kernel, base, target, (len(big) + len(unread), groups)),
        out_shape=out,
        in_specs=specs,
        out_specs=anywhere,
        scratch_shapes=scratch,
        input_output_aliases={len(operands) - 1: 0} if target == 0 else {},
        compiler_params=pltpu.CompilerParams(vmem_limit_bytes=VMEM_LIMIT),
        cost_estimate=pl.CostEstimate(flops=flops, bytes_accessed=6 * 2**20, transcendentals=10**7),
        name="two_frames",
    )(*operands)


def shards(frames, clip_frames, norm_gain, norm_bias, conv_weight, conv_bias, down_weight, down_bias):
    slabs, tiles = lax.axis_size("slab"), lax.axis_size("tile")
    both = ("slab", "tile")

    frames = pltpu.with_memory_space_constraint(frames, pltpu.HBM)
    sums, far, near, top, bottom = sums_and_rows(frames, slabs * tiles)
    sums = lax.all_to_all(sums, both, 0, 0)
    top = lax.ppermute(top, "tile", [(t, t + 1) for t in range(tiles - 1)])
    bottom = lax.ppermute(bottom, "tile", [(t + 1, t) for t in range(tiles - 1)])
    along = [(s, s + 1) for s in range(slabs - 1)]
    near = lax.ppermute(near, "slab", along)
    corners = [top[2:4].reshape(1, 2, *top.shape[2:]), bottom[2:4].reshape(1, 4, *bottom.shape[2:])]
    far = lax.dynamic_update_slice(far, jnp.concatenate(corners, axis=1), (0, 16, 0, 0))
    far = lax.ppermute(far, "slab", along)
    place = jnp.stack([lax.axis_index("slab"), lax.axis_index("tile"), jnp.int32(tiles)]).astype(jnp.int32)
    scalars, shared = jnp.concatenate([place, clip_frames]), (sums, conv_weight, down_weight)
    vectors = [v[None] for v in (norm_gain, norm_bias, conv_bias, down_bias)]
    last = two_frames(
        0, 2, scalars, vectors, shared, (frames, top, bottom), [(0, 4, (0, 0, 0), (1, 0, 0), (2, 0, 0))], FLOPS, (near,))
    groups = [
        (0, 1, (0, 0, 0), (0, 0, 16), (0, 0, 18)),
        (1, 1, (1, 0, 0), (0, 0, 17), (0, 0, 20)),
        (2, 2, (2, 0, 0), (3, 0, 0), (4, 0, 0)),
    ]
    return two_frames(-2, 0, scalars, vectors, shared, (far, near, frames, top, bottom), groups, FLOPS, (last,))


def solution(mesh):
    return jax.shard_map(
        shards,
        mesh=mesh,
        in_specs=(P("slab", "tile", None, None), P(), P(), P(), P(), P(), P(), P()),
        out_specs=P("slab", "tile", None, None),
        check_vma=False,
    )
```
